32 devices in a mesh: grp: 2 (over y), blk: 4 (over z), sub: 4 (over x, core).
Axes of the slice: x: 2, y: 2, z: 4, core: 2. Of those that a mesh axis runs over, the one named last changes fastest.
Arguments:
- acts: bfloat16 [32, 48, 5120], P(('grp', 'blk', 'sub')), parts along dimension 0, may hold values from -6 to 6
- outgrads: bfloat16 [32, 48, 6912], P(('grp', 'blk', 'sub')), parts along dimension 0, may hold values from -6 to 6
- moment: float32 [6912, 5120], P('blk'), may hold values from 12 to 192
- counts: int32 [32], P(('grp', 'blk', 'sub')), parts along dimension 0, may hold values from 1 to 48, 576 in all
- seeds: int32 [2], replicated, may hold values from 0 to 999999
Outputs:
- sketch: float32 [32, 512, 128], P(('grp', 'blk', 'sub')), parts along dimension 0
The draws below stay inside these ranges and needn't reach their ends.
There are 2 independent parts, one for each index of `grp`. The reference program is written for one: setup_inputs(seed, part) draws one part's arguments, and reference() takes and returns one part's arrays. A program takes and returns all parts, laid end to end along the dimension named above; an argument that names none is the same for every part. Nothing has to cross between parts.
Inputs may be any that keep to these rules, and one draw needn't show every extreme that they name: Each example has 1 to 48 live tokens; some example of each group has 48; the counts of one group's 16 examples sum to 3 * 16 * 48 // 4 (the printed array holds all groups one after another, each with this sum).
All inputs are finite; a program needn't handle non-finite values.
Results may differ from the reference program's by a relative error of at most 0.0042.
Values may be sent and summed in bfloat16 or wider, within the bound.
No kernel may reach another device: no remote copies, remote signals or barrier semaphores. Data moves between devices by JAX's collectives and lax.ppermute only.
A program may use at most 320 MiB of HBM per device.

```python
import math
import jax
import jax.numpy as jnp
import numpy as np
from jax import lax

D = 5120
FW = 6912
KR = 512
KC = 128
TOK = 48
EXAMPLES = 16


def shard_levels(own_key, shape, shards, low, high):
    level, own = 1.0, jax.random.fold_in(own_key, 6)
    for dim, shards_of in shards:
        steps = jnp.exp(jax.random.uniform(jax.random.fold_in(own, dim), (shards_of,), jnp.float32, low / len(shards), high / len(shards)))
        level = level * jnp.repeat(steps, shape[dim] // shards_of).reshape([-1 if axis == dim else 1 for axis in range(len(shape))])
    return level


def split_up(count, total, bound, lean):
    loads = [(1 << 20) // math.isqrt(rank ** lean) + 1 for rank in range(2, count + 1)]
    surplus, given = total - bound - (count - 1), [1] * (count - 1)
    while surplus > 0:
        candidates = [i for i in range(count - 1) if given[i] < bound]
        mass, left = sum([loads[i] for i in candidates]), surplus
        for i in candidates:
            extra = min(bound - given[i], max(1, left * loads[i] // mass), surplus)
            given[i] = given[i] + extra
            surplus = surplus - extra
    return np.array([bound] + given)


def uneven_parts(rng, number_of, total, most, skew):
    if number_of == 2:
        one = jax.random.randint(rng, (), max(1, total - most), min(most, total - 1) + 1)
        return jnp.stack([one, total - one])
    sizes = jnp.asarray(split_up(number_of, total, most, skew), jnp.int32)
    couples = (number_of - 1) // 2
    giver, receiver = sizes[1:1 + 2 * couples:2], sizes[2:2 + 2 * couples:2]
    room = jnp.minimum(giver - 1, most - receiver)
    passed = jax.random.randint(jax.random.fold_in(rng, 1), (couples,), 0, 1 << 20) % (room + 1)
    sizes = sizes.at[1:1 + 2 * couples:2].set(giver - passed).at[2:2 + 2 * couples:2].set(receiver + passed)
    return sizes[jax.random.permutation(jax.random.fold_in(rng, 2), number_of)]


def normal_values(key, dims, deviation, limit, cuts=(), held_as=jnp.bfloat16):
    result = deviation * jax.random.normal(key, dims, jnp.float32)
    if cuts:
        result = result * shard_levels(key, dims, cuts, -0.22, 0.18)
    return jnp.clip(result, -limit, limit).astype(held_as)


def setup_inputs(seed: int = 0, part: int = 0) -> dict:
    streams_of = jax.random.split(jax.random.key(seed), 6)
    part_splits = jax.random.split(jax.random.fold_in(streams_of[5], part), 6)
    acts = normal_values(part_splits[0], (EXAMPLES, TOK, D), 1.0, 6.0, ((0, 16),))
    outgrads = normal_values(part_splits[1], (EXAMPLES, TOK, FW), 1.0, 6.0, ((0, 16),))
    moment = jnp.clip(jnp.exp(math.log(192.0) - 2.7725887 * jax.random.uniform(streams_of[2], (FW, D), jnp.float32) ** shard_levels(streams_of[2], (FW, D), ((0, 4),), -0.2, 0.2)), 12.0, 192.0)
    counts = uneven_parts(part_splits[3], EXAMPLES, EXAMPLES * TOK * 3 // 4, TOK, 2).astype(jnp.int32)
    seeds = jax.random.randint(streams_of[4], (2,), 0, 1000000).astype(jnp.int32)
    return dict(acts=acts, outgrads=outgrads, moment=moment, counts=counts, seeds=seeds)


def rademacher(row_index, col_index, seed_value):
    hashed = row_index[:, None] * 1597334677 + col_index[None, :] * 668265263 + seed_value * 374761393
    hashed = hashed ^ hashed >> 15
    hashed = hashed * 1274126177
    hashed = hashed ^ hashed >> 13
    return (1 - 2 * (hashed >> 7 & 1)).astype(jnp.float32)

def reference(acts, outgrads, moment, counts, seeds):
    inside = jnp.arange(TOK, dtype=jnp.int32)[None, :] < counts[:, None]
    masked = jnp.where(inside[:, :, None], outgrads, jnp.zeros((), outgrads.dtype)).astype(jnp.bfloat16)
    row_proj = (rademacher(jnp.arange(FW, dtype=jnp.int32), jnp.arange(KR, dtype=jnp.int32), seeds[0]) / jnp.sqrt(jnp.float32(FW))).astype(jnp.bfloat16)
    col_proj = (rademacher(jnp.arange(D, dtype=jnp.int32), jnp.arange(KC, dtype=jnp.int32), seeds[1]) / jnp.sqrt(jnp.float32(D))).astype(jnp.bfloat16)
    weights = 1.0 / (jnp.sqrt(moment) + 1e-08)

    def single(operands):
        grad_rows, act_rows = operands
        gradient = jnp.dot(grad_rows.T, act_rows, preferred_element_type=jnp.float32)
        scaled = (gradient * weights).astype(jnp.bfloat16)
        partial_sum = jnp.dot(scaled, col_proj, preferred_element_type=jnp.float32).astype(jnp.bfloat16)
        return jnp.dot(row_proj.T, partial_sum, preferred_element_type=jnp.float32)
    return lax.map(single, (masked, acts))
```

```python
import functools
import math

import jax
import jax.numpy as jnp
import numpy as np
from jax import lax
from jax.experimental import pallas as pl
from jax.experimental.pallas import tpu as pltpu
from jax.sharding import PartitionSpec as P

D = 5120
FW = 6912
KR = 512
KC = 128
F32 = jnp.float32
BF16 = jnp.bfloat16
VMEM = pl.BlockSpec(memory_space=pltpu.VMEM)
SMEM = pl.BlockSpec(memory_space=pltpu.SMEM)
HBM = pl.BlockSpec(memory_space=pltpu.HBM)
LIMIT = 24 << 20


def rademacher(row_index, col_index, seed_value):
    hashed = (
        row_index[:, None] * 1597334677 + col_index[None, :] * 668265263 + seed_value * 374761393
    )
    hashed = hashed ^ hashed >> 15
    hashed = hashed * 1274126177
    hashed = hashed ^ hashed >> 13
    return (1 - 2 * (hashed >> 7 & 1)).astype(jnp.float32)


def generic_shards(acts, outgrads, moment, counts, seeds):
    row_count = moment.shape[0]
    inside = (
        lax.broadcasted_iota(jnp.int32, (acts.shape[0], acts.shape[1], 1), 1)
        < counts[:, None, None]
    )
    masked = jnp.where(inside, outgrads, jnp.zeros((), outgrads.dtype))
    rows_in = lax.all_to_all(masked, "blk", split_axis=2, concat_axis=0, tiled=True)
    offset = lax.axis_index("blk") * row_count
    col_proj = (
        rademacher(jnp.arange(D, dtype=jnp.int32), jnp.arange(KC, dtype=jnp.int32), seeds[1])
        / jnp.sqrt(jnp.float32(D))
    ).astype(jnp.bfloat16)
    weights = 1.0 / (jnp.sqrt(moment) + 1e-08)

    def partial_rows_of(grad_rows, act_rows):
        gradient = jnp.einsum(
            "etr,etd->erd", grad_rows, act_rows, preferred_element_type=jnp.float32
        )
        scaled = (gradient * weights[None]).astype(jnp.bfloat16)
        return jnp.einsum(
            "erd,dk->erk", scaled, col_proj, preferred_element_type=jnp.float32
        ).astype(jnp.bfloat16)

    def blocked(grad_rows, act_rows, method):
        number = grad_rows.shape[0]
        group = math.gcd(number, 4)
        if group == number:
            return method(grad_rows, act_rows)
        grad_groups = grad_rows.reshape((number // group, group) + grad_rows.shape[1:])
        act_groups = act_rows.reshape((number // group, group) + act_rows.shape[1:])
        results = lax.map(
            lambda operands: method(operands[0], operands[1]), (grad_groups, act_groups)
        )
        return results.reshape((number,) + results.shape[2:])

    row_proj = (
        rademacher(
            offset + jnp.arange(row_count, dtype=jnp.int32),
            jnp.arange(KR, dtype=jnp.int32),
            seeds[0],
        )
        / jnp.sqrt(jnp.float32(FW))
    ).astype(jnp.bfloat16)

    def project(grad_rows, act_rows):
        partial_sum = partial_rows_of(grad_rows, act_rows)
        return jnp.einsum("rj,erk->ejk", row_proj, partial_sum, preferred_element_type=jnp.float32)

    acts_all = lax.all_gather(acts, "blk", axis=0, tiled=True)
    terms = blocked(rows_in, acts_all, project)
    sketch = lax.psum_scatter(terms, "blk", scatter_dimension=0, tiled=True)
    return sketch


def hashed_sign(rows_part, cols_part, scale):
    h = rows_part + cols_part
    h = h ^ (h >> 15)
    h = h * 1274126177
    h = h ^ (h >> 13)
    return jnp.where(((h >> 7) & 1) == 0, scale, -scale).astype(BF16)


def iota_times(shape, axis, factor, first=0):
    return (lax.broadcasted_iota(jnp.int32, shape, axis) + first) * factor


def split_kernel(counts, place, grads, *outs):
    tokens = grads.shape[0]
    rows = outs[0].shape[1]
    live = lax.broadcasted_iota(jnp.int32, (tokens, rows), 0) < counts[0]
    for block in range(len(outs)):
        part = grads[:, block * rows : (block + 1) * rows]
        part = jnp.where(live, part.astype(F32), 0.0).astype(BF16)
        for k, out in enumerate(outs):

            @pl.when(place[0] == block ^ k)
            def _():
                out[...] = part


def project_rows(row_proj, partial, out):
    out[...] = jnp.dot(row_proj[...], partial[...], preferred_element_type=F32).astype(out.dtype)


def first_kernel(
    tile, chunk, seeds, place, grads, acts, moment, out, weights, col_proj, row_proj, grads_t, partial, sems
):
    rows, depth = weights.shape
    tiles = rows // tile

    def moment_copy(t):
        part = pl.ds(pl.multiple_of(t * tile, 16), tile)
        return pltpu.make_async_copy(moment.at[part], weights.at[part], sems.at[t])

    for t in range(tiles):
        moment_copy(t).start()
    row_scale, col_scale = (float(np.float32(1) / np.sqrt(np.float32(n))) for n in (FW, D))
    cols_part = iota_times((1, KC), 1, 668265263) + seeds[1] * 374761393

    @pl.loop(0, depth // 256)
    def _(c):
        part = pl.ds(pl.multiple_of(c * 256, 256), 256)
        rows_part = iota_times((256, 1), 0, 1597334677, c * 256)
        col_proj[part] = hashed_sign(rows_part, cols_part, col_scale)

    across = iota_times((1, rows), 1, 1597334677, place[0] * rows) + seeds[0] * 374761393

    @pl.loop(0, KR // 32)
    def _(j):
        part = pl.ds(pl.multiple_of(j * 32, 32), 32)
        down = iota_times((32, 1), 0, 668265263, j * 32)
        row_proj[part] = hashed_sign(down, across, row_scale)

    grads_t[...] = grads[...].astype(F32).T.astype(BF16)

    @pl.loop(0, tiles)
    def _(t):
        moment_copy(t).wait()
        part = pl.ds(pl.multiple_of(t * tile, 16), tile)
        left = grads_t[part]
        total = jnp.zeros((tile, KC), F32)
        for c in range(0, depth, chunk):
            cols = pl.ds(c, chunk)
            weight = weights[part, cols]
            weight = 1.0 / (weight * lax.rsqrt(weight) + 1e-08)
            weights[part, cols] = weight
            gradient = jnp.dot(left, acts[:, cols], preferred_element_type=F32)
            scaled = (gradient * weight).astype(BF16)
            total += jnp.dot(scaled, col_proj[cols], preferred_element_type=F32)
        partial[part] = total.astype(BF16)

    project_rows(row_proj, partial, out)


def next_kernel(tile, chunk, place, grads_m, grads_e, acts_m, acts_e, weights, col_proj, row_proj, out, acts, grads_t, partial):
    rows, depth = weights.shape
    tiles = rows // tile
    if grads_e is None:
        grads_t[...] = grads_m[...].astype(F32).T.astype(BF16)
        acts = acts_m
    else:
        middle = jnp.logical_or(place[0] == 1, place[0] == 2)

        @pl.when(middle)
        def _():
            acts[...] = acts_m[...]

        @pl.when(jnp.logical_not(middle))
        def _():
            acts[...] = acts_e[...]

        grads_t[...] = grads_m[...].astype(F32).T.astype(BF16)

    @pl.loop(0, tiles)
    def _(t):
        part = pl.ds(pl.multiple_of(t * tile, 16), tile)
        left = grads_t[part]
        total = jnp.zeros((tile, KC), F32)
        for c in range(0, depth, chunk):
            cols = pl.ds(c, chunk)
            gradient = jnp.dot(left, acts[:, cols], preferred_element_type=F32)
            scaled = (gradient * weights[part, cols]).astype(BF16)
            total += jnp.dot(scaled, col_proj[cols], preferred_element_type=F32)
        partial[part] = total.astype(BF16)

    project_rows(row_proj, partial, out)


def line_shards(acts, outgrads, moment, counts, seeds):
    rows, depth = moment.shape
    tokens = acts.shape[1]
    tile = rows // 4
    chunk = 256
    acts, outgrads = acts[0], outgrads[0]
    place = lax.axis_index("blk").astype(jnp.int32)[None]
    cost = pl.CostEstimate(flops=4 * rows * depth * 256, bytes_accessed=rows * depth * 4, transcendentals=0)
    params = pltpu.CompilerParams(vmem_limit_bytes=LIMIT)

    swap = [(0, 1), (1, 0), (2, 3), (3, 2)]
    two = [(0, 2), (2, 0), (1, 3), (3, 1)]
    three = [(0, 3), (3, 0), (1, 2), (2, 1)]
    inner = [(1, 2), (2, 1)]
    outward = [(2, 3), (1, 0)]

    def send(x, pairs):
        return lax.ppermute(x, "blk", pairs)

    near = send(acts, swap)
    across = send(acts, inner)
    own_g, near_g, two_g, three_g = pl.pallas_call(
        split_kernel,
        in_specs=[SMEM, SMEM, VMEM],
        out_specs=[VMEM] * 4,
        out_shape=[jax.ShapeDtypeStruct((tokens, rows), BF16)] * 4,
    )(counts, place, outgrads)
    near_g = send(near_g, swap)
    two_g = send(two_g, two)
    three_g = send(three_g, three)

    own, weights, col_proj, row_proj = pl.pallas_call(
        functools.partial(first_kernel, tile, chunk),
        in_specs=[SMEM, SMEM, VMEM, VMEM, HBM],
        out_specs=[VMEM] * 4,
        out_shape=[
            jax.ShapeDtypeStruct((KR, KC), F32),
            pltpu.VMEM((rows, depth), F32),
            pltpu.VMEM((depth, KC), BF16),
            pltpu.VMEM((KR, rows), BF16),
        ],
        scratch_shapes=[
            pltpu.VMEM((rows, tokens), BF16),
            pltpu.VMEM((rows, KC), BF16),
            pltpu.SemaphoreType.DMA((rows // tile,)),
        ],
        compiler_params=params,
        cost_estimate=cost,
    )(seeds, place, pltpu.with_memory_space_constraint(own_g, pltpu.VMEM), acts, moment)

    def held(x):
        return pltpu.with_memory_space_constraint(x, pltpu.VMEM)

    def term(grads, acts_m, acts_e=None):
        scratch = [pltpu.VMEM((rows, tokens), BF16), pltpu.VMEM((rows, KC), BF16)]
        common = dict(
            out_specs=VMEM,
            out_shape=jax.ShapeDtypeStruct((KR, KC), BF16),
            compiler_params=params,
            cost_estimate=cost,
        )
        if acts_e is None:

            def body(place, g, a, w, c, r, out, grads_t, partial):
                next_kernel(tile, chunk, place, g, None, a, None, w, c, r, out, None, grads_t, partial)

            return pl.pallas_call(body, in_specs=[SMEM] + [VMEM] * 5, scratch_shapes=scratch, **common)(
                place, held(grads), held(acts_m), held(weights), held(col_proj), held(row_proj)
            )

        def body(place, g, a, b, w, c, r, out, chosen, grads_t, partial):
            next_kernel(tile, chunk, place, g, g, a, b, w, c, r, out, chosen, grads_t, partial)

        return pl.pallas_call(
            body, in_specs=[SMEM] + [VMEM] * 6, scratch_shapes=[pltpu.VMEM((tokens, depth), BF16)] + scratch, **common
        )(place, held(grads), held(acts_m), held(acts_e), held(weights), held(col_proj), held(row_proj))

    near2 = send(near, inner)
    across2 = send(across, outward)
    near_term = send(term(near_g, near), swap)
    last = send(near2, outward)
    two_term = send(term(two_g, near2, across2), two)
    three_term = send(term(three_g, across, last), three)
    sketch = own + near_term.astype(F32) + two_term.astype(F32) + three_term.astype(F32)
    return sketch[None]


def solution(mesh):
    placed = (
        P(("grp", "blk", "sub"), None, None),
        P(("grp", "blk", "sub"), None, None),
        P("blk", None),
        P(("grp", "blk", "sub")),
        P(),
    )

    def shards(acts, outgrads, moment, counts, seeds):
        line = mesh.shape["blk"] == 4 and acts.shape[0] == 1 and moment.shape[0] % 64 == 0
        return (line_shards if line else generic_shards)(acts, outgrads, moment, counts, seeds)

    return jax.shard_map(
        shards,
        mesh=mesh,
        in_specs=placed,
        out_specs=P(("grp", "blk", "sub"), None, None),
        check_vma=False,
    )
```

```python
import functools
import math

import jax
import jax.numpy as jnp
import numpy as np
from jax import lax
from jax.experimental import pallas as pl
from jax.experimental.pallas import tpu as pltpu
from jax.sharding import PartitionSpec as P

D = 5120
FW = 6912
KR = 512
KC = 128
F32 = jnp.float32
BF16 = jnp.bfloat16
VMEM = pl.BlockSpec(memory_space=pltpu.VMEM)
SMEM = pl.BlockSpec(memory_space=pltpu.SMEM)
HBM = pl.BlockSpec(memory_space=pltpu.HBM)
LIMIT = 24 << 20


def rademacher(row_index, col_index, seed_value):
    hashed = (
        row_index[:, None] * 1597334677 + col_index[None, :] * 668265263 + seed_value * 374761393
    )
    hashed = hashed ^ hashed >> 15
    hashed = hashed * 1274126177
    hashed = hashed ^ hashed >> 13
    return (1 - 2 * (hashed >> 7 & 1)).astype(jnp.float32)


def generic_shards(acts, outgrads, moment, counts, seeds):
    row_count = moment.shape[0]
    inside = (
        lax.broadcasted_iota(jnp.int32, (acts.shape[0], acts.shape[1], 1), 1)
        < counts[:, None, None]
    )
    masked = jnp.where(inside, outgrads, jnp.zeros((), outgrads.dtype))
    rows_in = lax.all_to_all(masked, "blk", split_axis=2, concat_axis=0, tiled=True)
    offset = lax.axis_index("blk") * row_count
    col_proj = (
        rademacher(jnp.arange(D, dtype=jnp.int32), jnp.arange(KC, dtype=jnp.int32), seeds[1])
        / jnp.sqrt(jnp.float32(D))
    ).astype(jnp.bfloat16)
    weights = 1.0 / (jnp.sqrt(moment) + 1e-08)

    def partial_rows_of(grad_rows, act_rows):
        gradient = jnp.einsum(
            "etr,etd->erd", grad_rows, act_rows, preferred_element_type=jnp.float32
        )
        scaled = (gradient * weights[None]).astype(jnp.bfloat16)
        return jnp.einsum(
            "erd,dk->erk", scaled, col_proj, preferred_element_type=jnp.float32
        ).astype(jnp.bfloat16)

    def blocked(grad_rows, act_rows, method):
        number = grad_rows.shape[0]
        group = math.gcd(number, 4)
        if group == number:
            return method(grad_rows, act_rows)
        grad_groups = grad_rows.reshape((number // group, group) + grad_rows.shape[1:])
        act_groups = act_rows.reshape((number // group, group) + act_rows.shape[1:])
        results = lax.map(
            lambda operands: method(operands[0], operands[1]), (grad_groups, act_groups)
        )
        return results.reshape((number,) + results.shape[2:])

    row_proj = (
        rademacher(
            offset + jnp.arange(row_count, dtype=jnp.int32),
            jnp.arange(KR, dtype=jnp.int32),
            seeds[0],
        )
        / jnp.sqrt(jnp.float32(FW))
    ).astype(jnp.bfloat16)

    def project(grad_rows, act_rows):
        partial_sum = partial_rows_of(grad_rows, act_rows)
        return jnp.einsum("rj,erk->ejk", row_proj, partial_sum, preferred_element_type=jnp.float32)

    acts_all = lax.all_gather(acts, "blk", axis=0, tiled=True)
    terms = blocked(rows_in, acts_all, project)
    sketch = lax.psum_scatter(terms, "blk", scatter_dimension=0, tiled=True)
    return sketch


def hashed_sign(rows_part, cols_part, scale):
    h = rows_part + cols_part
    h = h ^ (h >> 15)
    h = h * 1274126177
    h = h ^ (h >> 13)
    return jnp.where(((h >> 7) & 1) == 0, scale, -scale).astype(BF16)


def iota_times(shape, axis, factor, first=0):
    return (lax.broadcasted_iota(jnp.int32, shape, axis) + first) * factor


def split_kernel(counts, place, grads, *outs):
    tokens = grads.shape[0]
    rows = outs[0].shape[1]
    live = lax.broadcasted_iota(jnp.int32, (tokens, rows), 0) < counts[0]
    for block in range(len(outs)):
        part = grads[:, block * rows : (block + 1) * rows]
        part = jnp.where(live, part.astype(F32), 0.0).astype(BF16)
        for k, out in enumerate(outs):

            @pl.when(place[0] == block ^ k)
            def _():
                out[...] = part


def project_rows(row_proj, partial, out):
    out[...] = jnp.dot(row_proj[...], partial[...], preferred_element_type=F32).astype(out.dtype)


def first_kernel(
    tile, chunk, seeds, place, grads, acts, moment, out, weights, col_proj, row_proj, grads_t, partial, sems
):
    rows, depth = weights.shape
    tiles = rows // tile

    def moment_copy(t):
        part = pl.ds(pl.multiple_of(t * tile, 16), tile)
        return pltpu.make_async_copy(moment.at[part], weights.at[part], sems.at[t])

    for t in range(tiles):
        moment_copy(t).start()
    row_scale, col_scale = (float(np.float32(1) / np.sqrt(np.float32(n))) for n in (FW, D))
    cols_part = iota_times((1, KC), 1, 668265263) + seeds[1] * 374761393

    @pl.loop(0, depth // 256)
    def _(c):
        part = pl.ds(pl.multiple_of(c * 256, 256), 256)
        rows_part = iota_times((256, 1), 0, 1597334677, c * 256)
        col_proj[part] = hashed_sign(rows_part, cols_part, col_scale)

    across = iota_times((1, rows), 1, 1597334677, place[0] * rows) + seeds[0] * 374761393

    @pl.loop(0, KR // 32)
    def _(j):
        part = pl.ds(pl.multiple_of(j * 32, 32), 32)
        down = iota_times((32, 1), 0, 668265263, j * 32)
        row_proj[part] = hashed_sign(down, across, row_scale)

    grads_t[...] = grads[...].astype(F32).T.astype(BF16)

    @pl.loop(0, tiles)
    def _(t):
        moment_copy(t).wait()
        part = pl.ds(pl.multiple_of(t * tile, 16), tile)
        left = grads_t[part]
        total = jnp.zeros((tile, KC), F32)
        for c in range(0, depth, chunk):
            cols = pl.ds(c, chunk)
            weight = weights[part, cols]
            weight = 1.0 / (weight * lax.rsqrt(weight) + 1e-08)
            weights[part, cols] = weight
            gradient = jnp.dot(left, acts[:, cols], preferred_element_type=F32)
            scaled = (gradient * weight).astype(BF16)
            total += jnp.dot(scaled, col_proj[cols], preferred_element_type=F32)
        partial[part] = total.astype(BF16)

    project_rows(row_proj, partial, out)


def next_kernel(tile, chunk, place, grads_m, grads_e, acts_m, acts_e, weights, col_proj, row_proj, out, acts, grads_t, partial):
    rows, depth = weights.shape
    tiles = rows // tile
    if grads_e is None:
        grads_t[...] = grads_m[...].astype(F32).T.astype(BF16)
        acts = acts_m
    else:
        middle = jnp.logical_or(place[0] == 1, place[0] == 2)

        @pl.when(middle)
        def _():
            acts[...] = acts_m[...]

        @pl.when(jnp.logical_not(middle))
        def _():
            acts[...] = acts_e[...]

        grads_t[...] = grads_m[...].astype(F32).T.astype(BF16)

    @pl.loop(0, tiles)
    def _(t):
        part = pl.ds(pl.multiple_of(t * tile, 16), tile)
        left = grads_t[part]
        total = jnp.zeros((tile, KC), F32)
        for c in range(0, depth, chunk):
            cols = pl.ds(c, chunk)
            gradient = jnp.dot(left, acts[:, cols], preferred_element_type=F32)
            scaled = (gradient * weights[part, cols]).astype(BF16)
            total += jnp.dot(scaled, col_proj[cols], preferred_element_type=F32)
        partial[part] = total.astype(BF16)

    project_rows(row_proj, partial, out)


def line_shards(acts, outgrads, moment, counts, seeds):
    rows, depth = moment.shape
    tokens = acts.shape[1]
    tile = rows // 4
    chunk = 256
    acts, outgrads = acts[0], outgrads[0]
    place = lax.axis_index("blk").astype(jnp.int32)[None]
    cost = pl.CostEstimate(flops=4 * rows * depth * 256, bytes_accessed=rows * depth * 4, transcendentals=0)
    params = pltpu.CompilerParams(vmem_limit_bytes=LIMIT)

    swap = [(0, 1), (1, 0), (2, 3), (3, 2)]
    two = [(0, 2), (2, 0), (1, 3), (3, 1)]
    three = [(0, 3), (3, 0), (1, 2), (2, 1)]
    inner = [(1, 2), (2, 1)]
    outward = [(2, 3), (1, 0)]

    def send(x, pairs):
        return lax.ppermute(x, "blk", pairs)

    near = send(acts, swap)
    across = send(acts, inner)
    own_g, near_g, two_g, three_g = pl.pallas_call(
        split_kernel,
        in_specs=[SMEM, SMEM, VMEM],
        out_specs=[VMEM] * 4,
        out_shape=[jax.ShapeDtypeStruct((tokens, rows), BF16)] * 4,
    )(counts, place, outgrads)
    near_g = send(near_g, swap)
    two_g = send(two_g, two)
    three_g = send(three_g, three)

    own, weights, col_proj, row_proj = pl.pallas_call(
        functools.partial(first_kernel, tile, chunk),
        in_specs=[SMEM, SMEM, VMEM, VMEM, HBM],
        out_specs=[VMEM] * 4,
        out_shape=[
            jax.ShapeDtypeStruct((KR, KC), F32),
            pltpu.VMEM((rows, depth), F32),
            pltpu.VMEM((depth, KC), BF16),
            pltpu.VMEM((KR, rows), BF16),
        ],
        scratch_shapes=[
            pltpu.VMEM((rows, tokens), BF16),
            pltpu.VMEM((rows, KC), BF16),
            pltpu.SemaphoreType.DMA((rows // tile,)),
        ],
        compiler_params=params,
        cost_estimate=cost,
    )(seeds, place, own_g, acts, moment)

    def held(x):
        return pltpu.with_memory_space_constraint(x, pltpu.VMEM)

    def term(grads, acts_m, acts_e=None):
        scratch = [pltpu.VMEM((rows, tokens), BF16), pltpu.VMEM((rows, KC), BF16)]
        common = dict(
            out_specs=VMEM,
            out_shape=jax.ShapeDtypeStruct((KR, KC), BF16),
            compiler_params=params,
            cost_estimate=cost,
        )
        if acts_e is None:

            def body(place, g, a, w, c, r, out, grads_t, partial):
                next_kernel(tile, chunk, place, g, None, a, None, w, c, r, out, None, grads_t, partial)

            return pl.pallas_call(body, in_specs=[SMEM] + [VMEM] * 5, scratch_shapes=scratch, **common)(
                place, held(grads), held(acts_m), held(weights), held(col_proj), held(row_proj)
            )

        def body(place, g, a, b, w, c, r, out, chosen, grads_t, partial):
            next_kernel(tile, chunk, place, g, g, a, b, w, c, r, out, chosen, grads_t, partial)

        return pl.pallas_call(
            body, in_specs=[SMEM] + [VMEM] * 6, scratch_shapes=[pltpu.VMEM((tokens, depth), BF16)] + scratch, **common
        )(place, held(grads), held(acts_m), held(acts_e), held(weights), held(col_proj), held(row_proj))

    near2 = send(near, inner)
    across2 = send(across, outward)
    near_term = send(term(near_g, near), swap)
    last = send(near2, outward)
    two_term = send(term(two_g, near2, across2), two)
    three_term = send(term(three_g, across, last), three)
    sketch = own + near_term.astype(F32) + two_term.astype(F32) + three_term.astype(F32)
    return sketch[None]


def solution(mesh):
    placed = (
        P(("grp", "blk", "sub"), None, None),
        P(("grp", "blk", "sub"), None, None),
        P("blk", None),
        P(("grp", "blk", "sub")),
        P(),
    )

    def shards(acts, outgrads, moment, counts, seeds):
        line = mesh.shape["blk"] == 4 and acts.shape[0] == 1 and moment.shape[0] % 64 == 0
        return (line_shards if line else generic_shards)(acts, outgrads, moment, counts, seeds)

    return jax.shard_map(
        shards,
        mesh=mesh,
        in_specs=placed,
        out_specs=P(("grp", "blk", "sub"), None, None),
        check_vma=False,
    )
```

```python
import functools
import math

import jax
import jax.numpy as jnp
import numpy as np
from jax import lax
from jax.experimental import pallas as pl
from jax.experimental.pallas import tpu as pltpu
from jax.sharding import PartitionSpec as P

D = 5120
FW = 6912
KR = 512
KC = 128
F32 = jnp.float32
BF16 = jnp.bfloat16
VMEM = pl.BlockSpec(memory_space=pltpu.VMEM)
SMEM = pl.BlockSpec(memory_space=pltpu.SMEM)
ANY = pl.BlockSpec(memory_space=pl.ANY)
HBM = pl.BlockSpec(memory_space=pltpu.HBM)
LIMIT = 24 << 20


def rademacher(row_index, col_index, seed_value):
    hashed = (
        row_index[:, None] * 1597334677 + col_index[None, :] * 668265263 + seed_value * 374761393
    )
    hashed = hashed ^ hashed >> 15
    hashed = hashed * 1274126177
    hashed = hashed ^ hashed >> 13
    return (1 - 2 * (hashed >> 7 & 1)).astype(jnp.float32)


def generic_shards(acts, outgrads, moment, counts, seeds):
    row_count = moment.shape[0]
    inside = (
        lax.broadcasted_iota(jnp.int32, (acts.shape[0], acts.shape[1], 1), 1)
        < counts[:, None, None]
    )
    masked = jnp.where(inside, outgrads, jnp.zeros((), outgrads.dtype))
    rows_in = lax.all_to_all(masked, "blk", split_axis=2, concat_axis=0, tiled=True)
    offset = lax.axis_index("blk") * row_count
    col_proj = (
        rademacher(jnp.arange(D, dtype=jnp.int32), jnp.arange(KC, dtype=jnp.int32), seeds[1])
        / jnp.sqrt(jnp.float32(D))
    ).astype(jnp.bfloat16)
    weights = 1.0 / (jnp.sqrt(moment) + 1e-08)

    def partial_rows_of(grad_rows, act_rows):
        gradient = jnp.einsum(
            "etr,etd->erd", grad_rows, act_rows, preferred_element_type=jnp.float32
        )
        scaled = (gradient * weights[None]).astype(jnp.bfloat16)
        return jnp.einsum(
            "erd,dk->erk", scaled, col_proj, preferred_element_type=jnp.float32
        ).astype(jnp.bfloat16)

    def blocked(grad_rows, act_rows, method):
        number = grad_rows.shape[0]
        group = math.gcd(number, 4)
        if group == number:
            return method(grad_rows, act_rows)
        grad_groups = grad_rows.reshape((number // group, group) + grad_rows.shape[1:])
        act_groups = act_rows.reshape((number // group, group) + act_rows.shape[1:])
        results = lax.map(
            lambda operands: method(operands[0], operands[1]), (grad_groups, act_groups)
        )
        return results.reshape((number,) + results.shape[2:])

    row_proj = (
        rademacher(
            offset + jnp.arange(row_count, dtype=jnp.int32),
            jnp.arange(KR, dtype=jnp.int32),
            seeds[0],
        )
        / jnp.sqrt(jnp.float32(FW))
    ).astype(jnp.bfloat16)

    def project(grad_rows, act_rows):
        partial_sum = partial_rows_of(grad_rows, act_rows)
        return jnp.einsum("rj,erk->ejk", row_proj, partial_sum, preferred_element_type=jnp.float32)

    acts_all = lax.all_gather(acts, "blk", axis=0, tiled=True)
    terms = blocked(rows_in, acts_all, project)
    sketch = lax.psum_scatter(terms, "blk", scatter_dimension=0, tiled=True)
    return sketch


def hashed_sign(rows_part, cols_part, scale):
    h = rows_part + cols_part
    h = h ^ (h >> 15)
    h = h * 1274126177
    h = h ^ (h >> 13)
    return jnp.where(((h >> 7) & 1) == 0, scale, -scale).astype(BF16)


def iota_times(shape, axis, factor, first=0):
    return (lax.broadcasted_iota(jnp.int32, shape, axis) + first) * factor


def split_kernel(counts, place, grads, *outs):
    tokens = grads.shape[0]
    rows = outs[0].shape[1]
    live = lax.broadcasted_iota(jnp.int32, (tokens, rows), 0) < counts[0]
    for block in range(len(outs)):
        part = grads[:, block * rows : (block + 1) * rows]
        part = jnp.where(live, part.astype(F32), 0.0).astype(BF16)
        for k, out in enumerate(outs):

            @pl.when(place[0] == block ^ k)
            def _():
                out[...] = part


def project_rows(row_proj, partial, out):
    out[...] = jnp.dot(row_proj[...], partial[...], preferred_element_type=F32).astype(out.dtype)


def first_kernel(
    tile, chunk, seeds, place, grads, acts, moment, out, weights, col_proj, row_proj, grads_t, partial, sems
):
    rows, depth = weights.shape
    tiles = rows // tile

    def moment_copy(t):
        part = pl.ds(pl.multiple_of(t * tile, 16), tile)
        return pltpu.make_async_copy(moment.at[part], weights.at[part], sems.at[t])

    for t in range(tiles):
        moment_copy(t).start()
    row_scale, col_scale = (float(np.float32(1) / np.sqrt(np.float32(n))) for n in (FW, D))
    cols_part = iota_times((1, KC), 1, 668265263) + seeds[1] * 374761393

    @pl.loop(0, depth // 256)
    def _(c):
        part = pl.ds(pl.multiple_of(c * 256, 256), 256)
        rows_part = iota_times((256, 1), 0, 1597334677, c * 256)
        col_proj[part] = hashed_sign(rows_part, cols_part, col_scale)

    across = iota_times((1, rows), 1, 1597334677, place[0] * rows) + seeds[0] * 374761393

    @pl.loop(0, KR // 32)
    def _(j):
        part = pl.ds(pl.multiple_of(j * 32, 32), 32)
        down = iota_times((32, 1), 0, 668265263, j * 32)
        row_proj[part] = hashed_sign(down, across, row_scale)

    grads_t[...] = grads[...].astype(F32).T.astype(BF16)

    @pl.loop(0, tiles)
    def _(t):
        moment_copy(t).wait()
        part = pl.ds(pl.multiple_of(t * tile, 16), tile)
        left = grads_t[part]
        total = jnp.zeros((tile, KC), F32)
        for c in range(0, depth, chunk):
            cols = pl.ds(c, chunk)
            weight = weights[part, cols]
            weight = 1.0 / (weight * lax.rsqrt(weight) + 1e-08)
            weights[part, cols] = weight
            gradient = jnp.dot(left, acts[:, cols], preferred_element_type=F32)
            scaled = (gradient * weight).astype(BF16)
            total += jnp.dot(scaled, col_proj[cols], preferred_element_type=F32)
        partial[part] = total.astype(BF16)

    project_rows(row_proj, partial, out)


def next_kernel(tile, chunk, place, grads_m, grads_e, acts_m, acts_e, weights, col_proj, row_proj, out, acts, grads_t, partial):
    rows, depth = weights.shape
    tiles = rows // tile
    if grads_e is None:
        grads_t[...] = grads_m[...].astype(F32).T.astype(BF16)
        acts = acts_m
    else:
        middle = jnp.logical_or(place[0] == 1, place[0] == 2)

        @pl.when(middle)
        def _():
            acts[...] = acts_m[...]

        @pl.when(jnp.logical_not(middle))
        def _():
            acts[...] = acts_e[...]

        grads_t[...] = grads_m[...].astype(F32).T.astype(BF16)

    @pl.loop(0, tiles)
    def _(t):
        part = pl.ds(pl.multiple_of(t * tile, 16), tile)
        left = grads_t[part]
        total = jnp.zeros((tile, KC), F32)
        for c in range(0, depth, chunk):
            cols = pl.ds(c, chunk)
            gradient = jnp.dot(left, acts[:, cols], preferred_element_type=F32)
            scaled = (gradient * weights[part, cols]).astype(BF16)
            total += jnp.dot(scaled, col_proj[cols], preferred_element_type=F32)
        partial[part] = total.astype(BF16)

    project_rows(row_proj, partial, out)


def line_shards(acts, outgrads, moment, counts, seeds):
    rows, depth = moment.shape
    tokens = acts.shape[1]
    tile = rows // 4
    chunk = 256
    acts, outgrads = acts[0], outgrads[0]
    place = lax.axis_index("blk").astype(jnp.int32)[None]
    cost = pl.CostEstimate(flops=4 * rows * depth * 256, bytes_accessed=rows * depth * 4, transcendentals=0)
    params = pltpu.CompilerParams(vmem_limit_bytes=LIMIT)

    swap = [(0, 1), (1, 0), (2, 3), (3, 2)]
    two = [(0, 2), (2, 0), (1, 3), (3, 1)]
    three = [(0, 3), (3, 0), (1, 2), (2, 1)]
    inner = [(1, 2), (2, 1)]
    outward = [(2, 3), (1, 0)]

    def send(x, pairs):
        return lax.ppermute(x, "blk", pairs)

    near = send(acts, swap)
    across = send(acts, inner)
    own_g, near_g, two_g, three_g = pl.pallas_call(
        split_kernel,
        in_specs=[SMEM, SMEM, VMEM],
        out_specs=[VMEM] * 4,
        out_shape=[jax.ShapeDtypeStruct((tokens, rows), BF16)] * 4,
    )(counts, place, outgrads)
    near_g = send(near_g, swap)
    two_g = send(two_g, two)
    three_g = send(three_g, three)

    own, weights, col_proj, row_proj = pl.pallas_call(
        functools.partial(first_kernel, tile, chunk),
        in_specs=[SMEM, SMEM, VMEM, VMEM, HBM],
        out_specs=[VMEM] * 4,
        out_shape=[
            jax.ShapeDtypeStruct((KR, KC), F32),
            pltpu.VMEM((rows, depth), F32),
            pltpu.VMEM((depth, KC), BF16),
            pltpu.VMEM((KR, rows), BF16),
        ],
        scratch_shapes=[
            pltpu.VMEM((rows, tokens), BF16),
            pltpu.VMEM((rows, KC), BF16),
            pltpu.SemaphoreType.DMA((rows // tile,)),
        ],
        compiler_params=params,
        cost_estimate=cost,
    )(seeds, place, own_g, acts, moment)

    def held(x):
        return pltpu.with_memory_space_constraint(x, pltpu.VMEM)

    def term(grads, acts_m, acts_e=None, through=None):
        scratch = [pltpu.VMEM((rows, tokens), BF16), pltpu.VMEM((rows, KC), BF16)]
        common = dict(
            out_specs=VMEM,
            out_shape=jax.ShapeDtypeStruct((KR, KC), BF16),
            compiler_params=params,
            cost_estimate=cost,
        )
        if acts_e is None:

            def body(place, g, a, w, c, r, out, grads_t, partial):
                next_kernel(rows // 2, chunk, place, g, None, a, None, w, c, r, out, None, grads_t, partial)

            return pl.pallas_call(body, in_specs=[SMEM] + [VMEM] * 5, scratch_shapes=scratch, **common)(
                place, held(grads), held(acts_m), held(weights), held(col_proj), held(row_proj)
            )

        def body(place, g, a, b, w, c, r, *refs):
            out, chosen, grads_t, partial = refs[1 if through is not None else 0], *refs[-3:]
            next_kernel(rows // 2, chunk, place, g, g, a, b, w, c, r, out, chosen, grads_t, partial)

        operands = (place, held(grads), held(acts_m), held(acts_e), held(weights), held(col_proj), held(row_proj))
        scratch = [pltpu.VMEM((tokens, depth), BF16)] + scratch
        if through is None:
            return pl.pallas_call(body, in_specs=[SMEM] + [VMEM] * 6, scratch_shapes=scratch, **common)(*operands)
        common["out_specs"] = [VMEM, ANY]
        common["out_shape"] = [common["out_shape"], jax.ShapeDtypeStruct(through.shape, through.dtype)]
        return pl.pallas_call(
            body,
            in_specs=[SMEM] + [VMEM] * 6 + [ANY],
            input_output_aliases={7: 1},
            scratch_shapes=scratch,
            **common,
        )(*operands, through)

    near2 = send(near, inner)
    across2 = send(across, outward)
    near_own = term(near_g, near)
    last = send(near2, outward)
    two_own, near_own = term(two_g, near2, across2, near_own)
    two_term = send(two_own, two)
    near_term = send(near_own, swap)
    three_term = send(term(three_g, across, last), three)
    sketch = own + near_term.astype(F32) + two_term.astype(F32) + three_term.astype(F32)
    return sketch[None]


def solution(mesh):
    placed = (
        P(("grp", "blk", "sub"), None, None),
        P(("grp", "blk", "sub"), None, None),
        P("blk", None),
        P(("grp", "blk", "sub")),
        P(),
    )

    def shards(acts, outgrads, moment, counts, seeds):
        line = mesh.shape["blk"] == 4 and acts.shape[0] == 1 and moment.shape[0] % 64 == 0
        return (line_shards if line else generic_shards)(acts, outgrads, moment, counts, seeds)

    return jax.shard_map(
        shards,
        mesh=mesh,
        in_specs=placed,
        out_specs=P(("grp", "blk", "sub"), None, None),
        check_vma=False,
    )
```

```python
import functools
import math

import jax
import jax.numpy as jnp
import numpy as np
from jax import lax
from jax.experimental import pallas as pl
from jax.experimental.pallas import tpu as pltpu
from jax.sharding import PartitionSpec as P

D = 5120
FW = 6912
KR = 512
KC = 128
F32 = jnp.float32
BF16 = jnp.bfloat16
VMEM = pl.BlockSpec(memory_space=pltpu.VMEM)
SMEM = pl.BlockSpec(memory_space=pltpu.SMEM)
ANY = pl.BlockSpec(memory_space=pl.ANY)
HBM = pl.BlockSpec(memory_space=pltpu.HBM)
LIMIT = 24 << 20


def rademacher(row_index, col_index, seed_value):
    hashed = (
        row_index[:, None] * 1597334677 + col_index[None, :] * 668265263 + seed_value * 374761393
    )
    hashed = hashed ^ hashed >> 15
    hashed = hashed * 1274126177
    hashed = hashed ^ hashed >> 13
    return (1 - 2 * (hashed >> 7 & 1)).astype(jnp.float32)


def generic_shards(acts, outgrads, moment, counts, seeds):
    row_count = moment.shape[0]
    inside = (
        lax.broadcasted_iota(jnp.int32, (acts.shape[0], acts.shape[1], 1), 1)
        < counts[:, None, None]
    )
    masked = jnp.where(inside, outgrads, jnp.zeros((), outgrads.dtype))
    rows_in = lax.all_to_all(masked, "blk", split_axis=2, concat_axis=0, tiled=True)
    offset = lax.axis_index("blk") * row_count
    col_proj = (
        rademacher(jnp.arange(D, dtype=jnp.int32), jnp.arange(KC, dtype=jnp.int32), seeds[1])
        / jnp.sqrt(jnp.float32(D))
    ).astype(jnp.bfloat16)
    weights = 1.0 / (jnp.sqrt(moment) + 1e-08)

    def partial_rows_of(grad_rows, act_rows):
        gradient = jnp.einsum(
            "etr,etd->erd", grad_rows, act_rows, preferred_element_type=jnp.float32
        )
        scaled = (gradient * weights[None]).astype(jnp.bfloat16)
        return jnp.einsum(
            "erd,dk->erk", scaled, col_proj, preferred_element_type=jnp.float32
        ).astype(jnp.bfloat16)

    def blocked(grad_rows, act_rows, method):
        number = grad_rows.shape[0]
        group = math.gcd(number, 4)
        if group == number:
            return method(grad_rows, act_rows)
        grad_groups = grad_rows.reshape((number // group, group) + grad_rows.shape[1:])
        act_groups = act_rows.reshape((number // group, group) + act_rows.shape[1:])
        results = lax.map(
            lambda operands: method(operands[0], operands[1]), (grad_groups, act_groups)
        )
        return results.reshape((number,) + results.shape[2:])

    row_proj = (
        rademacher(
            offset + jnp.arange(row_count, dtype=jnp.int32),
            jnp.arange(KR, dtype=jnp.int32),
            seeds[0],
        )
        / jnp.sqrt(jnp.float32(FW))
    ).astype(jnp.bfloat16)

    def project(grad_rows, act_rows):
        partial_sum = partial_rows_of(grad_rows, act_rows)
        return jnp.einsum("rj,erk->ejk", row_proj, partial_sum, preferred_element_type=jnp.float32)

    acts_all = lax.all_gather(acts, "blk", axis=0, tiled=True)
    terms = blocked(rows_in, acts_all, project)
    sketch = lax.psum_scatter(terms, "blk", scatter_dimension=0, tiled=True)
    return sketch


def hashed_sign(rows_part, cols_part, scale):
    h = rows_part + cols_part
    h = h ^ (h >> 15)
    h = h * 1274126177
    h = h ^ (h >> 13)
    return jnp.where(((h >> 7) & 1) == 0, scale, -scale).astype(BF16)


def iota_times(shape, axis, factor, first=0):
    return (lax.broadcasted_iota(jnp.int32, shape, axis) + first) * factor


def split_kernel(counts, place, grads, *outs):
    tokens = grads.shape[0]
    rows = outs[0].shape[1]
    live = lax.broadcasted_iota(jnp.int32, (tokens, rows), 0) < counts[0]
    for block in range(len(outs)):
        part = grads[:, block * rows : (block + 1) * rows]
        part = jnp.where(live, part.astype(F32), 0.0).astype(BF16)
        for k, out in enumerate(outs):

            @pl.when(place[0] == block ^ k)
            def _():
                out[...] = part


def project_rows(row_proj, partial, out):
    out[...] = jnp.dot(row_proj[...], partial[...], preferred_element_type=F32).astype(out.dtype)


def first_kernel(
    tile, chunk, seeds, place, grads, acts, moment, out, weights, col_proj, row_proj, grads_t, partial, sems
):
    rows, depth = weights.shape
    tiles = rows // tile

    def moment_copy(t):
        part = pl.ds(pl.multiple_of(t * tile, 16), tile)
        return pltpu.make_async_copy(moment.at[part], weights.at[part], sems.at[t])

    for t in range(tiles):
        moment_copy(t).start()
    row_scale, col_scale = (float(np.float32(1) / np.sqrt(np.float32(n))) for n in (FW, D))
    cols_part = iota_times((1, KC), 1, 668265263) + seeds[1] * 374761393

    @pl.loop(0, depth // 256)
    def _(c):
        part = pl.ds(pl.multiple_of(c * 256, 256), 256)
        rows_part = iota_times((256, 1), 0, 1597334677, c * 256)
        col_proj[part] = hashed_sign(rows_part, cols_part, col_scale)

    across = iota_times((1, rows), 1, 1597334677, place[0] * rows) + seeds[0] * 374761393

    @pl.loop(0, KR // 32)
    def _(j):
        part = pl.ds(pl.multiple_of(j * 32, 32), 32)
        down = iota_times((32, 1), 0, 668265263, j * 32)
        row_proj[part] = hashed_sign(down, across, row_scale)

    grads_t[...] = grads[...].astype(F32).T.astype(BF16)

    @pl.loop(0, tiles)
    def _(t):
        moment_copy(t).wait()
        part = pl.ds(pl.multiple_of(t * tile, 16), tile)
        left = grads_t[part]
        total = jnp.zeros((tile, KC), F32)
        for c in range(0, depth, chunk):
            cols = pl.ds(c, chunk)
            weight = weights[part, cols]
            weight = 1.0 / (weight * lax.rsqrt(weight) + 1e-08)
            weights[part, cols] = weight
            gradient = jnp.dot(left, acts[:, cols], preferred_element_type=F32)
            scaled = (gradient * weight).astype(BF16)
            total += jnp.dot(scaled, col_proj[cols], preferred_element_type=F32)
        partial[part] = total.astype(BF16)

    project_rows(row_proj, partial, out)


def next_kernel(tile, chunk, place, grads_m, grads_e, acts_m, acts_e, weights, col_proj, row_proj, out, acts, grads_t, partial, far=False):
    rows, depth = weights.shape
    tiles = rows // tile
    if grads_e is None:
        grads_t[...] = grads_m[...].astype(F32).T.astype(BF16)
        acts = acts_m
    else:
        middle = jnp.logical_or(place[0] == 1, place[0] == 2)

        @pl.when(middle)
        def _():
            if far:
                pltpu.sync_copy(acts_m, acts)
            else:
                acts[...] = acts_m[...]

        @pl.when(jnp.logical_not(middle))
        def _():
            acts[...] = acts_e[...]

        grads_t[...] = grads_m[...].astype(F32).T.astype(BF16)

    @pl.loop(0, tiles)
    def _(t):
        part = pl.ds(pl.multiple_of(t * tile, 16), tile)
        left = grads_t[part]
        total = jnp.zeros((tile, KC), F32)
        for c in range(0, depth, chunk):
            cols = pl.ds(c, chunk)
            gradient = jnp.dot(left, acts[:, cols], preferred_element_type=F32)
            scaled = (gradient * weights[part, cols]).astype(BF16)
            total += jnp.dot(scaled, col_proj[cols], preferred_element_type=F32)
        partial[part] = total.astype(BF16)

    project_rows(row_proj, partial, out)


def line_shards(acts, outgrads, moment, counts, seeds):
    rows, depth = moment.shape
    tokens = acts.shape[1]
    tile = rows // 4
    chunk = 256
    acts, outgrads = acts[0], outgrads[0]
    place = lax.axis_index("blk").astype(jnp.int32)[None]
    cost = pl.CostEstimate(flops=4 * rows * depth * 256, bytes_accessed=rows * depth * 4, transcendentals=0)
    params = pltpu.CompilerParams(vmem_limit_bytes=LIMIT)

    swap = [(0, 1), (1, 0), (2, 3), (3, 2)]
    two = [(0, 2), (2, 0), (1, 3), (3, 1)]
    three = [(0, 3), (3, 0), (1, 2), (2, 1)]
    inner = [(1, 2), (2, 1)]
    outward = [(2, 3), (1, 0)]

    def send(x, pairs):
        return lax.ppermute(x, "blk", pairs)

    near = send(acts, swap)
    across = send(acts, inner)
    own_g, near_g, two_g, three_g = pl.pallas_call(
        split_kernel,
        in_specs=[SMEM, SMEM, VMEM],
        out_specs=[VMEM] * 4,
        out_shape=[jax.ShapeDtypeStruct((tokens, rows), BF16)] * 4,
    )(counts, place, outgrads)
    near_g = send(near_g, swap)
    two_g = send(two_g, two)
    three_g = send(three_g, three)

    own, weights, col_proj, row_proj = pl.pallas_call(
        functools.partial(first_kernel, tile, chunk),
        in_specs=[SMEM, SMEM, VMEM, VMEM, HBM],
        out_specs=[VMEM] * 4,
        out_shape=[
            jax.ShapeDtypeStruct((KR, KC), F32),
            pltpu.VMEM((rows, depth), F32),
            pltpu.VMEM((depth, KC), BF16),
            pltpu.VMEM((KR, rows), BF16),
        ],
        scratch_shapes=[
            pltpu.VMEM((rows, tokens), BF16),
            pltpu.VMEM((rows, KC), BF16),
            pltpu.SemaphoreType.DMA((rows // tile,)),
        ],
        compiler_params=params,
        cost_estimate=cost,
    )(seeds, place, own_g, acts, moment)

    def held(x):
        return pltpu.with_memory_space_constraint(x, pltpu.VMEM)

    def term(grads, acts_m, acts_e=None, through=None):
        scratch = [pltpu.VMEM((rows, tokens), BF16), pltpu.VMEM((rows, KC), BF16)]
        common = dict(
            out_specs=VMEM,
            out_shape=jax.ShapeDtypeStruct((KR, KC), BF16),
            compiler_params=params,
            cost_estimate=cost,
        )
        if acts_e is None:

            def body(place, g, a, w, c, r, out, grads_t, partial):
                next_kernel(rows // 2, chunk, place, g, None, a, None, w, c, r, out, None, grads_t, partial)

            return pl.pallas_call(body, in_specs=[SMEM] + [VMEM] * 5, scratch_shapes=scratch, **common)(
                place, held(grads), held(acts_m), held(weights), held(col_proj), held(row_proj)
            )

        def body(place, g, a, b, w, c, r, *refs):
            out, chosen, grads_t, partial = refs[1 if through is not None else 0], *refs[-3:]
            next_kernel(rows // 2, chunk, place, g, g, a, b, w, c, r, out, chosen, grads_t, partial, through is None)

        operands = (place, held(grads), acts_m if through is None else held(acts_m), held(acts_e), held(weights), held(col_proj), held(row_proj))
        scratch = [pltpu.VMEM((tokens, depth), BF16)] + scratch
        if through is None:
            return pl.pallas_call(
                body, in_specs=[SMEM, VMEM, ANY] + [VMEM] * 4, scratch_shapes=scratch, **common
            )(*operands)
        common["out_specs"] = [VMEM, ANY]
        common["out_shape"] = [common["out_shape"], jax.ShapeDtypeStruct(through.shape, through.dtype)]
        return pl.pallas_call(
            body,
            in_specs=[SMEM] + [VMEM] * 6 + [ANY],
            input_output_aliases={7: 1},
            scratch_shapes=scratch,
            **common,
        )(*operands, through)

    near2 = send(near, inner)
    across2 = send(across, outward)
    near_own = term(near_g, near)
    last = send(near2, outward)
    two_own, near_own = term(two_g, near2, across2, near_own)
    two_term = send(two_own, two)
    near_term = send(near_own, swap)
    three_term = send(term(three_g, across, last), three)
    sketch = own + near_term.astype(F32) + two_term.astype(F32) + three_term.astype(F32)
    return sketch[None]


def solution(mesh):
    placed = (
        P(("grp", "blk", "sub"), None, None),
        P(("grp", "blk", "sub"), None, None),
        P("blk", None),
        P(("grp", "blk", "sub")),
        P(),
    )

    def shards(acts, outgrads, moment, counts, seeds):
        line = mesh.shape["blk"] == 4 and acts.shape[0] == 1 and moment.shape[0] % 64 == 0
        return (line_shards if line else generic_shards)(acts, outgrads, moment, counts, seeds)

    return jax.shard_map(
        shards,
        mesh=mesh,
        in_specs=placed,
        out_specs=P(("grp", "blk", "sub"), None, None),
        check_vma=False,
    )
```

```python
import functools
import math

import jax
import jax.numpy as jnp
import numpy as np
from jax import lax
from jax.experimental import pallas as pl
from jax.experimental.pallas import tpu as pltpu
from jax.sharding import PartitionSpec as P

D = 5120
FW = 6912
KR = 512
KC = 128
F32 = jnp.float32
BF16 = jnp.bfloat16
VMEM = pl.BlockSpec(memory_space=pltpu.VMEM)
SMEM = pl.BlockSpec(memory_space=pltpu.SMEM)
ANY = pl.BlockSpec(memory_space=pl.ANY)
HBM = pl.BlockSpec(memory_space=pltpu.HBM)
LIMIT = 24 << 20


def rademacher(row_index, col_index, seed_value):
    hashed = (
        row_index[:, None] * 1597334677 + col_index[None, :] * 668265263 + seed_value * 374761393
    )
    hashed = hashed ^ hashed >> 15
    hashed = hashed * 1274126177
    hashed = hashed ^ hashed >> 13
    return (1 - 2 * (hashed >> 7 & 1)).astype(jnp.float32)


def generic_shards(acts, outgrads, moment, counts, seeds):
    row_count = moment.shape[0]
    inside = (
        lax.broadcasted_iota(jnp.int32, (acts.shape[0], acts.shape[1], 1), 1)
        < counts[:, None, None]
    )
    masked = jnp.where(inside, outgrads, jnp.zeros((), outgrads.dtype))
    rows_in = lax.all_to_all(masked, "blk", split_axis=2, concat_axis=0, tiled=True)
    offset = lax.axis_index("blk") * row_count
    col_proj = (
        rademacher(jnp.arange(D, dtype=jnp.int32), jnp.arange(KC, dtype=jnp.int32), seeds[1])
        / jnp.sqrt(jnp.float32(D))
    ).astype(jnp.bfloat16)
    weights = 1.0 / (jnp.sqrt(moment) + 1e-08)

    def partial_rows_of(grad_rows, act_rows):
        gradient = jnp.einsum(
            "etr,etd->erd", grad_rows, act_rows, preferred_element_type=jnp.float32
        )
        scaled = (gradient * weights[None]).astype(jnp.bfloat16)
        return jnp.einsum(
            "erd,dk->erk", scaled, col_proj, preferred_element_type=jnp.float32
        ).astype(jnp.bfloat16)

    def blocked(grad_rows, act_rows, method):
        number = grad_rows.shape[0]
        group = math.gcd(number, 4)
        if group == number:
            return method(grad_rows, act_rows)
        grad_groups = grad_rows.reshape((number // group, group) + grad_rows.shape[1:])
        act_groups = act_rows.reshape((number // group, group) + act_rows.shape[1:])
        results = lax.map(
            lambda operands: method(operands[0], operands[1]), (grad_groups, act_groups)
        )
        return results.reshape((number,) + results.shape[2:])

    row_proj = (
        rademacher(
            offset + jnp.arange(row_count, dtype=jnp.int32),
            jnp.arange(KR, dtype=jnp.int32),
            seeds[0],
        )
        / jnp.sqrt(jnp.float32(FW))
    ).astype(jnp.bfloat16)

    def project(grad_rows, act_rows):
        partial_sum = partial_rows_of(grad_rows, act_rows)
        return jnp.einsum("rj,erk->ejk", row_proj, partial_sum, preferred_element_type=jnp.float32)

    acts_all = lax.all_gather(acts, "blk", axis=0, tiled=True)
    terms = blocked(rows_in, acts_all, project)
    sketch = lax.psum_scatter(terms, "blk", scatter_dimension=0, tiled=True)
    return sketch


def hashed_sign(rows_part, cols_part, scale):
    h = rows_part + cols_part
    h = h ^ (h >> 15)
    h = h * 1274126177
    h = h ^ (h >> 13)
    return jnp.where(((h >> 7) & 1) == 0, scale, -scale).astype(BF16)


def iota_times(shape, axis, factor, first=0):
    return (lax.broadcasted_iota(jnp.int32, shape, axis) + first) * factor


def split_kernel(counts, place, grads, *outs):
    tokens = grads.shape[0]
    rows = outs[0].shape[1]
    live = lax.broadcasted_iota(jnp.int32, (tokens, rows), 0) < counts[0]
    for block in range(len(outs)):
        part = grads[:, block * rows : (block + 1) * rows]
        part = jnp.where(live, part.astype(F32), 0.0).astype(BF16)
        for k, out in enumerate(outs):

            @pl.when(place[0] == block ^ k)
            def _():
                out[...] = part


def project_rows(row_proj, partial, out):
    out[...] = jnp.dot(row_proj[...], partial[...], preferred_element_type=F32).astype(out.dtype)


def first_kernel(
    tile, chunk, seeds, place, grads, acts, moment, out, weights, col_proj, row_proj, grads_t, partial, sems
):
    rows, depth = weights.shape
    tiles = rows // tile

    def moment_copy(t):
        part = pl.ds(pl.multiple_of(t * tile, 16), tile)
        return pltpu.make_async_copy(moment.at[part], weights.at[part], sems.at[t])

    for t in range(tiles):
        moment_copy(t).start()
    row_scale, col_scale = (float(np.float32(1) / np.sqrt(np.float32(n))) for n in (FW, D))
    cols_part = iota_times((1, KC), 1, 668265263) + seeds[1] * 374761393

    @pl.loop(0, depth // 256)
    def _(c):
        part = pl.ds(pl.multiple_of(c * 256, 256), 256)
        rows_part = iota_times((256, 1), 0, 1597334677, c * 256)
        col_proj[part] = hashed_sign(rows_part, cols_part, col_scale)

    across = iota_times((1, rows), 1, 1597334677, place[0] * rows) + seeds[0] * 374761393

    @pl.loop(0, KR // 32)
    def _(j):
        part = pl.ds(pl.multiple_of(j * 32, 32), 32)
        down = iota_times((32, 1), 0, 668265263, j * 32)
        row_proj[part] = hashed_sign(down, across, row_scale)

    grads_t[...] = grads[...].astype(F32).T.astype(BF16)

    @pl.loop(0, tiles)
    def _(t):
        moment_copy(t).wait()
        part = pl.ds(pl.multiple_of(t * tile, 16), tile)
        left = grads_t[part]
        total = jnp.zeros((tile, KC), F32)
        for c in range(0, depth, chunk):
            cols = pl.ds(c, chunk)
            weight = weights[part, cols]
            weight = 1.0 / (weight * lax.rsqrt(weight) + 1e-08)
            weights[part, cols] = weight
            gradient = jnp.dot(left, acts[:, cols], preferred_element_type=F32)
            scaled = (gradient * weight).astype(BF16)
            total += jnp.dot(scaled, col_proj[cols], preferred_element_type=F32)
        partial[part] = total.astype(BF16)

    project_rows(row_proj, partial, out)


def next_kernel(tile, chunk, place, grads_m, grads_e, acts_m, acts_e, weights, col_proj, row_proj, out, acts, grads_t, partial, far=False):
    rows, depth = weights.shape
    tiles = rows // tile
    if grads_e is None:
        grads_t[...] = grads_m[...].astype(F32).T.astype(BF16)
        acts = acts_m
    else:
        middle = jnp.logical_or(place[0] == 1, place[0] == 2)

        @pl.when(middle)
        def _():
            if far:
                pltpu.sync_copy(acts_m, acts)
            else:
                acts[...] = acts_m[...]

        @pl.when(jnp.logical_not(middle))
        def _():
            acts[...] = acts_e[...]

        grads_t[...] = grads_m[...].astype(F32).T.astype(BF16)

    cut = -(-(rows // 2) // 128) * 128
    sketch = jnp.zeros((KR, KC), F32)
    for begin, end in ((0, cut), (cut, rows)):
        part = pl.ds(begin, end - begin)
        left = grads_t[part]
        total = jnp.zeros((end - begin, KC), F32)
        for c in range(0, depth, chunk):
            cols = pl.ds(c, chunk)
            gradient = jnp.dot(left, acts[:, cols], preferred_element_type=F32)
            scaled = (gradient * weights[part, cols]).astype(BF16)
            total += jnp.dot(scaled, col_proj[cols], preferred_element_type=F32)
        sketch += jnp.dot(row_proj[:, begin:end], total.astype(BF16), preferred_element_type=F32)
    out[...] = sketch.astype(out.dtype)


def line_shards(acts, outgrads, moment, counts, seeds):
    rows, depth = moment.shape
    tokens = acts.shape[1]
    tile = rows // 4
    chunk = 256
    acts, outgrads = acts[0], outgrads[0]
    place = lax.axis_index("blk").astype(jnp.int32)[None]
    cost = pl.CostEstimate(flops=4 * rows * depth * 256, bytes_accessed=rows * depth * 4, transcendentals=0)
    params = pltpu.CompilerParams(vmem_limit_bytes=LIMIT)

    swap = [(0, 1), (1, 0), (2, 3), (3, 2)]
    two = [(0, 2), (2, 0), (1, 3), (3, 1)]
    three = [(0, 3), (3, 0), (1, 2), (2, 1)]
    inner = [(1, 2), (2, 1)]
    outward = [(2, 3), (1, 0)]

    def send(x, pairs):
        return lax.ppermute(x, "blk", pairs)

    near = send(acts, swap)
    across = send(acts, inner)
    own_g, near_g, two_g, three_g = pl.pallas_call(
        split_kernel,
        in_specs=[SMEM, SMEM, VMEM],
        out_specs=[VMEM] * 4,
        out_shape=[jax.ShapeDtypeStruct((tokens, rows), BF16)] * 4,
    )(counts, place, outgrads)
    near_g = send(near_g, swap)
    two_g = send(two_g, two)
    three_g = send(three_g, three)

    own, weights, col_proj, row_proj = pl.pallas_call(
        functools.partial(first_kernel, tile, chunk),
        in_specs=[SMEM, SMEM, VMEM, VMEM, HBM],
        out_specs=[VMEM] * 4,
        out_shape=[
            jax.ShapeDtypeStruct((KR, KC), F32),
            pltpu.VMEM((rows, depth), F32),
            pltpu.VMEM((depth, KC), BF16),
            pltpu.VMEM((KR, rows), BF16),
        ],
        scratch_shapes=[
            pltpu.VMEM((rows, tokens), BF16),
            pltpu.VMEM((rows, KC), BF16),
            pltpu.SemaphoreType.DMA((rows // tile,)),
        ],
        compiler_params=params,
        cost_estimate=cost,
    )(seeds, place, own_g, acts, moment)

    def held(x):
        return pltpu.with_memory_space_constraint(x, pltpu.VMEM)

    def term(grads, acts_m, acts_e=None, through=None):
        scratch = [pltpu.VMEM((rows, tokens), BF16), pltpu.VMEM((rows, KC), BF16)]
        common = dict(
            out_specs=VMEM,
            out_shape=jax.ShapeDtypeStruct((KR, KC), BF16),
            compiler_params=params,
            cost_estimate=cost,
        )
        if acts_e is None:

            def body(place, g, a, w, c, r, out, grads_t, partial):
                next_kernel(rows // 2, chunk, place, g, None, a, None, w, c, r, out, None, grads_t, partial)

            return pl.pallas_call(body, in_specs=[SMEM] + [VMEM] * 5, scratch_shapes=scratch, **common)(
                place, held(grads), held(acts_m), held(weights), held(col_proj), held(row_proj)
            )

        def body(place, g, a, b, w, c, r, *refs):
            out, chosen, grads_t, partial = refs[1 if through is not None else 0], *refs[-3:]
            next_kernel(rows // 2, chunk, place, g, g, a, b, w, c, r, out, chosen, grads_t, partial, through is None)

        operands = (place, held(grads), acts_m if through is None else held(acts_m), held(acts_e), held(weights), held(col_proj), held(row_proj))
        scratch = [pltpu.VMEM((tokens, depth), BF16)] + scratch
        if through is None:
            return pl.pallas_call(
                body, in_specs=[SMEM, VMEM, ANY] + [VMEM] * 4, scratch_shapes=scratch, **common
            )(*operands)
        common["out_specs"] = [VMEM, ANY]
        common["out_shape"] = [common["out_shape"], jax.ShapeDtypeStruct(through.shape, through.dtype)]
        return pl.pallas_call(
            body,
            in_specs=[SMEM] + [VMEM] * 6 + [ANY],
            input_output_aliases={7: 1},
            scratch_shapes=scratch,
            **common,
        )(*operands, through)

    near2 = send(near, inner)
    across2 = send(across, outward)
    near_own = term(near_g, near)
    last = send(near2, outward)
    two_own, near_own = term(two_g, near2, across2, near_own)
    two_term = send(two_own, two)
    near_term = send(near_own, swap)
    three_term = send(term(three_g, across, last), three)
    sketch = own + near_term.astype(F32) + two_term.astype(F32) + three_term.astype(F32)
    return sketch[None]


def solution(mesh):
    placed = (
        P(("grp", "blk", "sub"), None, None),
        P(("grp", "blk", "sub"), None, None),
        P("blk", None),
        P(("grp", "blk", "sub")),
        P(),
    )

    def shards(acts, outgrads, moment, counts, seeds):
        line = mesh.shape["blk"] == 4 and acts.shape[0] == 1 and moment.shape[0] % 64 == 0
        return (line_shards if line else generic_shards)(acts, outgrads, moment, counts, seeds)

    return jax.shard_map(
        shards,
        mesh=mesh,
        in_specs=placed,
        out_specs=P(("grp", "blk", "sub"), None, None),
        check_vma=False,
    )
```

```python
import functools
import math

import jax
import jax.numpy as jnp
import numpy as np
from jax import lax
from jax.experimental import pallas as pl
from jax.experimental.pallas import tpu as pltpu
from jax.sharding import PartitionSpec as P

D = 5120
FW = 6912
KR = 512
KC = 128
F32 = jnp.float32
BF16 = jnp.bfloat16
VMEM = pl.BlockSpec(memory_space=pltpu.VMEM)
SMEM = pl.BlockSpec(memory_space=pltpu.SMEM)
ANY = pl.BlockSpec(memory_space=pl.ANY)
HBM = pl.BlockSpec(memory_space=pltpu.HBM)
LIMIT = 24 << 20


def rademacher(row_index, col_index, seed_value):
    hashed = (
        row_index[:, None] * 1597334677 + col_index[None, :] * 668265263 + seed_value * 374761393
    )
    hashed = hashed ^ hashed >> 15
    hashed = hashed * 1274126177
    hashed = hashed ^ hashed >> 13
    return (1 - 2 * (hashed >> 7 & 1)).astype(jnp.float32)


def generic_shards(acts, outgrads, moment, counts, seeds):
    row_count = moment.shape[0]
    inside = (
        lax.broadcasted_iota(jnp.int32, (acts.shape[0], acts.shape[1], 1), 1)
        < counts[:, None, None]
    )
    masked = jnp.where(inside, outgrads, jnp.zeros((), outgrads.dtype))
    rows_in = lax.all_to_all(masked, "blk", split_axis=2, concat_axis=0, tiled=True)
    offset = lax.axis_index("blk") * row_count
    col_proj = (
        rademacher(jnp.arange(D, dtype=jnp.int32), jnp.arange(KC, dtype=jnp.int32), seeds[1])
        / jnp.sqrt(jnp.float32(D))
    ).astype(jnp.bfloat16)
    weights = 1.0 / (jnp.sqrt(moment) + 1e-08)

    def partial_rows_of(grad_rows, act_rows):
        gradient = jnp.einsum(
            "etr,etd->erd", grad_rows, act_rows, preferred_element_type=jnp.float32
        )
        scaled = (gradient * weights[None]).astype(jnp.bfloat16)
        return jnp.einsum(
            "erd,dk->erk", scaled, col_proj, preferred_element_type=jnp.float32
        ).astype(jnp.bfloat16)

    def blocked(grad_rows, act_rows, method):
        number = grad_rows.shape[0]
        group = math.gcd(number, 4)
        if group == number:
            return method(grad_rows, act_rows)
        grad_groups = grad_rows.reshape((number // group, group) + grad_rows.shape[1:])
        act_groups = act_rows.reshape((number // group, group) + act_rows.shape[1:])
        results = lax.map(
            lambda operands: method(operands[0], operands[1]), (grad_groups, act_groups)
        )
        return results.reshape((number,) + results.shape[2:])

    row_proj = (
        rademacher(
            offset + jnp.arange(row_count, dtype=jnp.int32),
            jnp.arange(KR, dtype=jnp.int32),
            seeds[0],
        )
        / jnp.sqrt(jnp.float32(FW))
    ).astype(jnp.bfloat16)

    def project(grad_rows, act_rows):
        partial_sum = partial_rows_of(grad_rows, act_rows)
        return jnp.einsum("rj,erk->ejk", row_proj, partial_sum, preferred_element_type=jnp.float32)

    acts_all = lax.all_gather(acts, "blk", axis=0, tiled=True)
    terms = blocked(rows_in, acts_all, project)
    sketch = lax.psum_scatter(terms, "blk", scatter_dimension=0, tiled=True)
    return sketch


def hashed_sign(rows_part, cols_part, scale):
    h = rows_part + cols_part
    h = h ^ (h >> 15)
    h = h * 1274126177
    h = h ^ (h >> 13)
    return jnp.where(((h >> 7) & 1) == 0, scale, -scale).astype(BF16)


def iota_times(shape, axis, factor, first=0):
    return (lax.broadcasted_iota(jnp.int32, shape, axis) + first) * factor


def split_kernel(counts, place, grads, *outs):
    tokens = grads.shape[0]
    rows = outs[0].shape[1]
    live = lax.broadcasted_iota(jnp.int32, (tokens, 1), 0) < counts[0]
    live = jnp.where(live, 1.0, 0.0).astype(BF16)
    for block in range(len(outs)):
        part = grads[:, block * rows : (block + 1) * rows]
        part = part * live
        for k, out in enumerate(outs):

            @pl.when(place[0] == block ^ k)
            def _():
                out[...] = part


def project_rows(row_proj, partial, out):
    out[...] = jnp.dot(row_proj[...], partial[...], preferred_element_type=F32).astype(out.dtype)


def first_kernel(
    tile, chunk, seeds, place, grads, acts, moment, out, weights, col_proj, row_proj, grads_t, partial, sems
):
    rows, depth = weights.shape
    tiles = rows // tile

    def moment_copy(t):
        part = pl.ds(pl.multiple_of(t * tile, 16), tile)
        return pltpu.make_async_copy(moment.at[part], weights.at[part], sems.at[t])

    for t in range(tiles):
        moment_copy(t).start()
    row_scale, col_scale = (float(np.float32(1) / np.sqrt(np.float32(n))) for n in (FW, D))
    cols_part = iota_times((1, KC), 1, 668265263) + seeds[1] * 374761393

    @pl.loop(0, depth // 256)
    def _(c):
        part = pl.ds(pl.multiple_of(c * 256, 256), 256)
        rows_part = iota_times((256, 1), 0, 1597334677, c * 256)
        col_proj[part] = hashed_sign(rows_part, cols_part, col_scale)

    across = iota_times((1, rows), 1, 1597334677, place[0] * rows) + seeds[0] * 374761393

    @pl.loop(0, KR // 32)
    def _(j):
        part = pl.ds(pl.multiple_of(j * 32, 32), 32)
        down = iota_times((32, 1), 0, 668265263, j * 32)
        row_proj[part] = hashed_sign(down, across, row_scale)

    grads_t[...] = grads[...].astype(F32).T.astype(BF16)

    @pl.loop(0, tiles)
    def _(t):
        moment_copy(t).wait()
        part = pl.ds(pl.multiple_of(t * tile, 16), tile)
        left = grads_t[part]
        total = jnp.zeros((tile, KC), F32)
        for c in range(0, depth, chunk):
            cols = pl.ds(c, chunk)
            weight = weights[part, cols]
            weight = 1.0 / (weight * lax.rsqrt(weight) + 1e-08)
            weights[part, cols] = weight
            gradient = jnp.dot(left, acts[:, cols], preferred_element_type=F32)
            scaled = (gradient * weight).astype(BF16)
            total += jnp.dot(scaled, col_proj[cols], preferred_element_type=F32)
        partial[part] = total.astype(BF16)

    project_rows(row_proj, partial, out)


def next_kernel(tile, chunk, place, grads_m, grads_e, acts_m, acts_e, weights, col_proj, row_proj, out, acts, grads_t, partial, far=False):
    rows, depth = weights.shape
    tiles = rows // tile
    if grads_e is None:
        grads_t[...] = grads_m[...].astype(F32).T.astype(BF16)
        acts = acts_m
    else:
        middle = jnp.logical_or(place[0] == 1, place[0] == 2)

        @pl.when(middle)
        def _():
            if far:
                pltpu.sync_copy(acts_m, acts)
            else:
                acts[...] = acts_m[...]

        @pl.when(jnp.logical_not(middle))
        def _():
            acts[...] = acts_e[...]

        grads_t[...] = grads_m[...].astype(F32).T.astype(BF16)

    cut = -(-(rows // 2) // 128) * 128
    sketch = jnp.zeros((KR, KC), F32)
    for begin, end in ((0, cut), (cut, rows)):
        part = pl.ds(begin, end - begin)
        left = grads_t[part]
        total = jnp.zeros((end - begin, KC), F32)
        for c in range(0, depth, chunk):
            cols = pl.ds(c, chunk)
            gradient = jnp.dot(left, acts[:, cols], preferred_element_type=F32)
            scaled = (gradient * weights[part, cols]).astype(BF16)
            total += jnp.dot(scaled, col_proj[cols], preferred_element_type=F32)
        sketch += jnp.dot(row_proj[:, begin:end], total.astype(BF16), preferred_element_type=F32)
    out[...] = sketch.astype(out.dtype)


def line_shards(acts, outgrads, moment, counts, seeds):
    rows, depth = moment.shape
    tokens = acts.shape[1]
    tile = rows // 4
    chunk = 256
    acts, outgrads = acts[0], outgrads[0]
    place = lax.axis_index("blk").astype(jnp.int32)[None]
    cost = pl.CostEstimate(flops=4 * rows * depth * 256, bytes_accessed=rows * depth * 4, transcendentals=0)
    params = pltpu.CompilerParams(vmem_limit_bytes=LIMIT)

    swap = [(0, 1), (1, 0), (2, 3), (3, 2)]
    two = [(0, 2), (2, 0), (1, 3), (3, 1)]
    three = [(0, 3), (3, 0), (1, 2), (2, 1)]
    inner = [(1, 2), (2, 1)]
    outward = [(2, 3), (1, 0)]

    def send(x, pairs):
        return lax.ppermute(x, "blk", pairs)

    near = send(acts, swap)
    across = send(acts, inner)
    own_g, near_g, two_g, three_g = pl.pallas_call(
        split_kernel,
        in_specs=[SMEM, SMEM, VMEM],
        out_specs=[VMEM] * 4,
        out_shape=[jax.ShapeDtypeStruct((tokens, rows), BF16)] * 4,
    )(counts, place, outgrads)
    near_g = send(near_g, swap)
    two_g = send(two_g, two)
    three_g = send(three_g, three)

    own, weights, col_proj, row_proj = pl.pallas_call(
        functools.partial(first_kernel, tile, chunk),
        in_specs=[SMEM, SMEM, VMEM, VMEM, HBM],
        out_specs=[VMEM] * 4,
        out_shape=[
            jax.ShapeDtypeStruct((KR, KC), F32),
            pltpu.VMEM((rows, depth), F32),
            pltpu.VMEM((depth, KC), BF16),
            pltpu.VMEM((KR, rows), BF16),
        ],
        scratch_shapes=[
            pltpu.VMEM((rows, tokens), BF16),
            pltpu.VMEM((rows, KC), BF16),
            pltpu.SemaphoreType.DMA((rows // tile,)),
        ],
        compiler_params=params,
        cost_estimate=cost,
    )(seeds, place, own_g, acts, moment)

    def held(x):
        return pltpu.with_memory_space_constraint(x, pltpu.VMEM)

    def term(grads, acts_m, acts_e=None, through=None):
        scratch = [pltpu.VMEM((rows, tokens), BF16), pltpu.VMEM((rows, KC), BF16)]
        common = dict(
            out_specs=VMEM,
            out_shape=jax.ShapeDtypeStruct((KR, KC), BF16),
            compiler_params=params,
            cost_estimate=cost,
        )
        if acts_e is None:

            def body(place, g, a, w, c, r, out, grads_t, partial):
                next_kernel(rows // 2, chunk, place, g, None, a, None, w, c, r, out, None, grads_t, partial)

            return pl.pallas_call(body, in_specs=[SMEM] + [VMEM] * 5, scratch_shapes=scratch, **common)(
                place, held(grads), held(acts_m), held(weights), held(col_proj), held(row_proj)
            )

        def body(place, g, a, b, w, c, r, *refs):
            out, chosen, grads_t, partial = refs[1 if through is not None else 0], *refs[-3:]
            next_kernel(rows // 2, chunk, place, g, g, a, b, w, c, r, out, chosen, grads_t, partial, through is None)

        operands = (place, held(grads), acts_m if through is None else held(acts_m), held(acts_e), held(weights), held(col_proj), held(row_proj))
        scratch = [pltpu.VMEM((tokens, depth), BF16)] + scratch
        if through is None:
            return pl.pallas_call(
                body, in_specs=[SMEM, VMEM, ANY] + [VMEM] * 4, scratch_shapes=scratch, **common
            )(*operands)
        common["out_specs"] = [VMEM, ANY]
        common["out_shape"] = [common["out_shape"], jax.ShapeDtypeStruct(through.shape, through.dtype)]
        return pl.pallas_call(
            body,
            in_specs=[SMEM] + [VMEM] * 6 + [ANY],
            input_output_aliases={7: 1},
            scratch_shapes=scratch,
            **common,
        )(*operands, through)

    near2 = send(near, inner)
    across2 = send(across, outward)
    near_own = term(near_g, near)
    last = send(near2, outward)
    two_own, near_own = term(two_g, near2, across2, near_own)
    two_term = send(two_own, two)
    near_term = send(near_own, swap)
    three_term = send(term(three_g, across, last), three)
    sketch = own + near_term.astype(F32) + two_term.astype(F32) + three_term.astype(F32)
    return sketch[None]


def solution(mesh):
    placed = (
        P(("grp", "blk", "sub"), None, None),
        P(("grp", "blk", "sub"), None, None),
        P("blk", None),
        P(("grp", "blk", "sub")),
        P(),
    )

    def shards(acts, outgrads, moment, counts, seeds):
        line = mesh.shape["blk"] == 4 and acts.shape[0] == 1 and moment.shape[0] % 64 == 0
        return (line_shards if line else generic_shards)(acts, outgrads, moment, counts, seeds)

    return jax.shard_map(
        shards,
        mesh=mesh,
        in_specs=placed,
        out_specs=P(("grp", "blk", "sub"), None, None),
        check_vma=False,
    )
```
